128 devices in a mesh: seq: 16 (over x, y), shard: 8 (over z, core).
Axes of the slice: x: 4, y: 4, z: 4, core: 2. Of those that a mesh axis runs over, the one named last changes fastest.
Arguments:
- tokens: bfloat16 [8192, 2560], P('seq'), may hold values from -6 to 6
- cotangent: bfloat16 [8192, 2560], P('seq'), may hold values from -6 to 6
- doc_bounds: int32 [3], replicated, may hold values from 0 to 8191, as said below
- branch_w: float32 [2, 2560, 10, 256], P(None, 'seq', None, 'shard'), may hold values from -0.125 to 0.125
- branch_m: float32 [2, 2560, 10, 256], P(None, 'seq', None, 'shard'), may hold values from -32 to 32
- branch_v: float32 [2, 2560, 10, 256], P(None, 'seq', None, 'shard'), may hold values from 155.648 to 622.592
- out_w: float32 [10, 256, 2560], P(None, 'shard', 'seq'), may hold values from -0.375 to 0.375
- out_m: float32 [10, 256, 2560], P(None, 'shard', 'seq'), may hold values from -32 to 32
- out_v: float32 [10, 256, 2560], P(None, 'shard', 'seq'), may hold values from 107.80672 to 430.8992
- gate_w: float32 [2, 10, 256, 256], P(None, None, 'seq', 'shard'), may hold values from -0.375 to 0.375
- gate_m: float32 [2, 10, 256, 256], P(None, None, 'seq', 'shard'), may hold values from -6 to 6
- gate_v: float32 [2, 10, 256, 256], P(None, None, 'seq', 'shard'), may hold values from 4.308992 to 17.2032
- mlp_w: float32 [2, 2560, 7680], P(None, 'seq', 'shard'), may hold values from -0.125 to 0.125
- mlp_m: float32 [2, 2560, 7680], P(None, 'seq', 'shard'), may hold values from -24 to 24
- mlp_v: float32 [2, 2560, 7680], P(None, 'seq', 'shard'), may hold values from 68.97664 to 276.0704
- down_w: float32 [7680, 2560], P('shard', 'seq'), may hold values from -0.125 to 0.125
- down_m: float32 [7680, 2560], P('shard', 'seq'), may hold values from -32 to 32
- down_v: float32 [7680, 2560], P('shard', 'seq'), may hold values from 107.80672 to 430.8992
- chan_w: float32 [8, 10, 256], P(None, None, ('shard', 'seq'))
- chan_m: float32 [8, 10, 256], P(None, None, ('shard', 'seq')), may hold values from -32 to 32
- chan_v: float32 [8, 10, 256], P(None, None, ('shard', 'seq')), may hold values from 107.80672 to 430.8992
- gains_w: float32 [2, 2560], P(None, 'seq'), may hold values from 0.1 to 1.9
- gains_m: float32 [2, 2560], P(None, 'seq'), may hold values from -64 to 64
- gains_v: float32 [2, 2560], P(None, 'seq'), may hold values from 430.8992 to 1720.32
Outputs:
- block_out: bfloat16 [8192, 2560], P('seq')
- token_grad: float32 [8192, 2560], P('seq')
- branch_first: float32 [2, 2560, 10, 256], P(None, 'seq', None, 'shard')
- branch_second: float32 [2, 2560, 10, 256], P(None, 'seq', None, 'shard')
- branch_new: float32 [2, 2560, 10, 256], P(None, 'seq', None, 'shard')
- out_first: float32 [10, 256, 2560], P(None, 'shard', 'seq')
- out_second: float32 [10, 256, 2560], P(None, 'shard', 'seq')
- out_new: float32 [10, 256, 2560], P(None, 'shard', 'seq')
- gate_first: float32 [2, 10, 256, 256], P(None, None, 'seq', 'shard')
- gate_second: float32 [2, 10, 256, 256], P(None, None, 'seq', 'shard')
- gate_new: float32 [2, 10, 256, 256], P(None, None, 'seq', 'shard')
- mlp_first: float32 [2, 2560, 7680], P(None, 'seq', 'shard')
- mlp_second: float32 [2, 2560, 7680], P(None, 'seq', 'shard')
- mlp_new: float32 [2, 2560, 7680], P(None, 'seq', 'shard')
- down_first: float32 [7680, 2560], P('shard', 'seq')
- down_second: float32 [7680, 2560], P('shard', 'seq')
- down_new: float32 [7680, 2560], P('shard', 'seq')
- chan_first: float32 [8, 10, 256], P(None, None, ('shard', 'seq'))
- chan_second: float32 [8, 10, 256], P(None, None, ('shard', 'seq'))
- chan_new: float32 [8, 10, 256], P(None, None, ('shard', 'seq'))
- gains_first: float32 [2, 2560], P(None, 'seq')
- gains_second: float32 [2, 2560], P(None, 'seq')
- gains_new: float32 [2, 2560], P(None, 'seq')
The draws below stay inside these ranges and needn't reach their ends.
Inputs may be any that keep to these rules, and one draw needn't show every extreme that they name: doc_bounds rises strictly: its first entry is 0, its second lies among the first 512 positions and its third among the last 512 positions.
All inputs are finite; a program needn't handle non-finite values.
Results may differ from the reference program's by a relative error of at most 0.007.
The reference program's roundings to bfloat16 on the way count: a program that leaves them out, or rounds other values in their place, can miss the bound.
Values may be sent and summed in bfloat16 or wider, within the bound.
A program may use at most 256 MiB of HBM per device.

```python
import math
from functools import partial
import jax
import jax.numpy as jnp
from jax import lax

D = 2560
H = 10
HS = 256
FF = 7680
CONV = 4
STEP = 5
TOK_DEV = 512
TOKENS = 8192


def draw_doc_bounds(key, part):
    key = jax.random.fold_in(key, 7)
    key_inner, key_outer = jax.random.split(key)
    inner_start = jax.random.randint(key_inner, (1,), 1, TOK_DEV)
    outer_start = jax.random.randint(key_outer, (1,), TOKENS - TOK_DEV + 1, TOKENS)
    return jnp.concatenate([jnp.zeros((1,), jnp.int32), inner_start.astype(jnp.int32), outer_start.astype(jnp.int32)]).astype(jnp.int32)


def draw_chan_w(key, part):
    key = jax.random.fold_in(key, 13)
    subkeys = jax.random.split(key, 5)
    slow_share = 0.5
    tap_scale = 0.8
    tap_draw = tap_scale * jax.random.normal(subkeys[0], (CONV, H, HS), jnp.float32)
    conv_bias = 0.6 * jax.random.normal(subkeys[1], (1, H, HS), jnp.float32)
    gate_bias = jax.random.normal(subkeys[2], (2, H, HS), jnp.float32)
    slow_mask = jax.random.bernoulli(subkeys[3], slow_share, (H, HS))
    factor = jnp.exp(jax.random.uniform(subkeys[4], (H, HS), jnp.float32, -0.6931, 0.6931))
    step_rate = jnp.where(slow_mask, factor / (8.0 * TOKENS), factor / 160.0)
    lam_row = jnp.log(jnp.expm1(step_rate))
    return jnp.concatenate([tap_draw, conv_bias, gate_bias, lam_row[None]], axis=0).astype(jnp.float32)


def steps_of(key, extent, pieces, least, high):
    def one(axis_at, blocks):
        draws = jax.random.uniform(jax.random.fold_in(jax.random.fold_in(key, 6), axis_at), (blocks,), jnp.float32, least / len(pieces), high / len(pieces))
        return jnp.repeat(jnp.exp(draws), extent[axis_at] // blocks).reshape((-1,) + (1,) * (len(extent) - axis_at - 1))

    factor_of = one(*pieces[0])
    for cut in pieces[1:]:
        factor_of = factor_of * one(*cut)
    return factor_of


def centred(rng, shape, deviation, limit, cuts=(), kind=jnp.bfloat16):
    entries = deviation * jax.random.normal(rng, shape, jnp.float32)
    if cuts:
        entries = entries * steps_of(rng, shape, cuts, -0.22, 0.18)
    return jnp.clip(entries, -limit, limit).astype(kind)


def setup_inputs(seed: int = 0) -> dict:
    key_list = jax.random.split(jax.random.key(seed), 25)
    return {
        "tokens": centred(key_list[0], (TOKENS, D), 1.0, 6.0, ((0, 16),)),
        "cotangent": centred(key_list[1], (TOKENS, D), 1.0, 6.0, ((0, 16),)),
        "doc_bounds": draw_doc_bounds(jax.random.fold_in(key_list[24], 71), 0),
        "branch_w": centred(key_list[3], (2, D, H, HS), D ** -0.5, 0.125, ((1, 16), (3, 8)), jnp.float32),
        "branch_m": centred(key_list[4], (2, D, H, HS), (0.0667 * TOKENS ** 0.5), 32.0, ((1, 16), (3, 8)), jnp.float32),
        "branch_v": jnp.clip(jnp.exp(math.log(622.592) - 1.3862944 * jax.random.uniform(key_list[5], (2, D, H, HS), jnp.float32) ** steps_of(key_list[5], (2, D, H, HS), ((1, 16), (3, 8)), -0.2, 0.2)), 155.648, 622.592),
        "out_w": centred(key_list[6], (H, HS, D), (H * HS // 9) ** -0.5, 0.375, ((1, 8), (2, 16)), jnp.float32),
        "out_m": centred(key_list[7], (H, HS, D), (0.0556 * TOKENS ** 0.5), 32.0, ((1, 8), (2, 16)), jnp.float32),
        "out_v": jnp.clip(jnp.exp(math.log(430.8992) - 1.3855342 * jax.random.uniform(key_list[8], (H, HS, D), jnp.float32) ** steps_of(key_list[8], (H, HS, D), ((1, 8), (2, 16)), -0.2, 0.2)), 107.80672, 430.8992),
        "gate_w": centred(key_list[9], (2, H, HS, HS), HS ** -0.5, 0.375, ((2, 16), (3, 8)), jnp.float32),
        "gate_m": centred(key_list[10], (2, H, HS, HS), (0.0111 * TOKENS ** 0.5), 6.0, ((2, 16), (3, 8)), jnp.float32),
        "gate_v": jnp.clip(jnp.exp(math.log(17.2032) - 1.3843914 * jax.random.uniform(key_list[11], (2, H, HS, HS), jnp.float32) ** steps_of(key_list[11], (2, H, HS, HS), ((2, 16), (3, 8)), -0.2, 0.2)), 4.308992, 17.2032),
        "mlp_w": centred(key_list[12], (2, D, FF), D ** -0.5, 0.125, ((1, 16), (2, 8)), jnp.float32),
        "mlp_m": centred(key_list[13], (2, D, FF), (0.0444 * TOKENS ** 0.5), 24.0, ((1, 16), (2, 8)), jnp.float32),
        "mlp_v": jnp.clip(jnp.exp(math.log(276.0704) - 1.386888 * jax.random.uniform(key_list[14], (2, D, FF), jnp.float32) ** steps_of(key_list[14], (2, D, FF), ((1, 16), (2, 8)), -0.2, 0.2)), 68.97664, 276.0704),
        "down_w": centred(key_list[15], (FF, D), (FF // 3) ** -0.5, 0.125, ((0, 8), (1, 16)), jnp.float32),
        "down_m": centred(key_list[16], (FF, D), (0.0556 * TOKENS ** 0.5), 32.0, ((0, 8), (1, 16)), jnp.float32),
        "down_v": jnp.clip(jnp.exp(math.log(430.8992) - 1.3855342 * jax.random.uniform(key_list[17], (FF, D), jnp.float32) ** steps_of(key_list[17], (FF, D), ((0, 8), (1, 16)), -0.2, 0.2)), 107.80672, 430.8992),
        "chan_w": draw_chan_w(jax.random.fold_in(key_list[24], 71), 0),
        "chan_m": centred(key_list[19], (CONV + 4, H, HS), (0.0556 * TOKENS ** 0.5), 32.0, ((2, 128),), jnp.float32),
        "chan_v": jnp.clip(jnp.exp(math.log(430.8992) - 1.3855342 * jax.random.uniform(key_list[20], (CONV + 4, H, HS), jnp.float32) ** steps_of(key_list[20], (CONV + 4, H, HS), ((2, 128),), -0.2, 0.2)), 107.80672, 430.8992),
        "gains_w": jnp.clip(1.0 + 0.18 * jax.random.normal(key_list[21], (2, D), jnp.float32), 0.1, 1.9),
        "gains_m": centred(key_list[22], (2, D), (0.111 * TOKENS ** 0.5), 64.0, ((1, 16),), jnp.float32),
        "gains_v": jnp.clip(jnp.exp(math.log(1720.32) - 1.3843914 * jax.random.uniform(key_list[23], (2, D), jnp.float32) ** steps_of(key_list[23], (2, D), ((1, 16),), -0.2, 0.2)), 430.8992, 1720.32),
    }


@jax.custom_vjp
def low(v):
    return lax.optimization_barrier(v.astype(jnp.bfloat16)).astype(jnp.float32)

@jax.custom_vjp
def low_back(v):
    return v

def low_keep(v):
    return (low(v), None)

def low_pass(kept, grad):
    return (grad,)

def back_keep(v):
    return (v, None)

def back_low(kept, grad):
    return (low(grad),)
low.defvjp(low_keep, low_pass)
low_back.defvjp(back_keep, back_low)
norm_eps = 1e-06
adam_eps = 1e-08
beta_one = 0.9
beta_two = 0.95
matrix_rate = 0.02
matrix_decay = 0.1
vector_rate = 1.0
gain_rate = 0.2

def rms_scale(row_block, gain_row):
    return row_block * lax.rsqrt(lax.optimization_barrier(jnp.mean(row_block * row_block, axis=-1, keepdims=True)) + norm_eps) * gain_row

def gelu_fn(values):
    return jax.nn.gelu(values, approximate=True)

def combine_pair(first_map, second_map):
    return (first_map[0] * second_map[0], second_map[0] * first_map[1] + second_map[1])

def tap_mask(positions, bounds):
    starts = lax.optimization_barrier(jnp.max(jnp.where(bounds[None, :] <= positions[:, None], bounds[None, :], 0), axis=1))
    offsets = jnp.arange(CONV, dtype=jnp.int32)
    return (positions[:, None] - offsets[None, :] >= starts[:, None]).astype(jnp.float32)

def conv_apply(padded, tap_table, kernel, row_count):
    summed = jnp.zeros((row_count,) + padded.shape[1:], jnp.float32)
    for offset in range(CONV):
        lead_row = CONV - 1 - offset
        summed = summed + tap_table[:, offset, None, None] * kernel[offset] * padded[lead_row:lead_row + row_count]
    return summed

def gate_piece(conv_out, pre_decay, pre_input, lam_row, reset_mask):
    gate_decay = jax.nn.sigmoid(pre_decay)
    gate_input = jax.nn.sigmoid(pre_input)
    log_decay = -8.0 * gate_decay * jax.nn.softplus(lam_row)
    norm_scale = jnp.where(reset_mask > 0, 1.0, jnp.sqrt(-jnp.expm1(2.0 * log_decay)))
    return (jnp.exp(log_decay) * (1.0 - reset_mask), conv_out * gate_input * norm_scale)

def adam_step(weight, moment_one, moment_two, gradient, step_rate, weight_decay):
    first_new = beta_one * moment_one + (1.0 - beta_one) * gradient
    second_new = beta_two * moment_two + (1.0 - beta_two) * gradient * gradient
    bias_one = 1.0 - beta_one ** STEP
    bias_two = 1.0 - beta_two ** STEP
    update = first_new / bias_one / (jnp.sqrt(second_new / bias_two) + adam_eps) + weight_decay * weight
    return (first_new, second_new, weight - step_rate * update)

def matmul(left_side, right_side):
    return jnp.dot(left_side, right_side, precision=lax.Precision.HIGHEST, preferred_element_type=jnp.float32)

def forward(tokens, branch_w, out_w, gate_w, mlp_w, down_w, chan_w, gains_w, doc_bounds):
    branch_w = low(branch_w)
    out_w = low(out_w)
    gate_w = low(gate_w)
    mlp_w = low(mlp_w)
    down_w = low(down_w)
    chan_w = low(chan_w)
    gains_w = low(gains_w)
    row_count = tokens.shape[0]
    positions = jnp.arange(row_count, dtype=jnp.int32)
    reset_mask = jnp.any(doc_bounds[None, :] == positions[:, None], axis=1).astype(jnp.float32)[:, None, None]
    tap_table = tap_mask(positions, doc_bounds)
    normed = low(rms_scale(tokens, gains_w[0]))
    branch_x = low_back(low(matmul(normed, branch_w[0].reshape(D, H * HS)))).reshape(row_count, H, HS)
    branch_y = low_back(matmul(normed, branch_w[1].reshape(D, H * HS))).reshape(row_count, H, HS)
    padded = jnp.concatenate([jnp.zeros((CONV - 1, H, HS), jnp.float32), branch_x], axis=0)
    conv_out = low_back(conv_apply(padded, tap_table, chan_w[0:CONV], row_count) + chan_w[CONV])
    gate_in = low(conv_out)
    gate_pre = low_back(jnp.einsum('thi,ghij->gthj', gate_in, gate_w, precision=lax.Precision.HIGHEST))
    decay_rate, inflow = gate_piece(conv_out, gate_pre[0] + chan_w[CONV + 1], gate_pre[1] + chan_w[CONV + 2], chan_w[CONV + 3], reset_mask)
    _, lru_state = lax.associative_scan(combine_pair, (decay_rate, inflow), axis=0)
    mixed_out = low(lru_state * gelu_fn(branch_y)).reshape(row_count, H * HS)
    middle = tokens + low_back(matmul(mixed_out, out_w.reshape(H * HS, D)))
    normed_two = low(rms_scale(middle, gains_w[1]))
    gate_val = low_back(matmul(normed_two, mlp_w[0]))
    up_val = low_back(matmul(normed_two, mlp_w[1]))
    hidden = low(gelu_fn(gate_val) * up_val)
    return middle + low_back(matmul(hidden, down_w))

def reference(tokens, cotangent, doc_bounds, branch_w, branch_m, branch_v, out_w, out_m, out_v, gate_w, gate_m, gate_v, mlp_w, mlp_m, mlp_v, down_w, down_m, down_v, chan_w, chan_m, chan_v, gains_w, gains_m, gains_v):
    block_out, back_fn = jax.vjp(partial(forward, doc_bounds=doc_bounds), tokens.astype(jnp.float32), branch_w, out_w, gate_w, mlp_w, down_w, chan_w, gains_w)
    token_grad, d_branch, d_out, d_gate, d_mlp, d_down, d_chan, d_gains = back_fn(cotangent.astype(jnp.float32))
    branch_first, branch_second, branch_new = adam_step(branch_w, branch_m, branch_v, d_branch, matrix_rate, matrix_decay)
    out_first, out_second, out_new = adam_step(out_w, out_m, out_v, d_out, matrix_rate, matrix_decay)
    gate_first, gate_second, gate_new = adam_step(gate_w, gate_m, gate_v, d_gate, matrix_rate, matrix_decay)
    mlp_first, mlp_second, mlp_new = adam_step(mlp_w, mlp_m, mlp_v, d_mlp, matrix_rate, matrix_decay)
    down_first, down_second, down_new = adam_step(down_w, down_m, down_v, d_down, matrix_rate, matrix_decay)
    chan_first, chan_second, chan_new = adam_step(chan_w, chan_m, chan_v, d_chan, vector_rate, 0.0)
    gains_first, gains_second, gains_new = adam_step(gains_w, gains_m, gains_v, d_gains, gain_rate, 0.0)
    return (block_out.astype(jnp.bfloat16), token_grad, branch_first, branch_second, branch_new, out_first, out_second, out_new, gate_first, gate_second, gate_new, mlp_first, mlp_second, mlp_new, down_first, down_second, down_new, chan_first, chan_second, chan_new, gains_first, gains_second, gains_new)
```

```python
from functools import partial

import jax
import jax.numpy as jnp
from jax import lax
from jax.experimental import pallas as pl
from jax.experimental.pallas import tpu as pltpu
from jax.sharding import PartitionSpec as P

CONV = 4
STEP = 5
BF = jnp.bfloat16
F32 = jnp.float32
MESH = pl.DeviceIdType.MESH
NX = 4
NZ = 4

norm_eps = 1e-06
adam_eps = 1e-08
beta_one = 0.9
beta_two = 0.95
matrix_rate = 0.02
matrix_decay = 0.1
vector_rate = 1.0
gain_rate = 0.2

ANY = pl.BlockSpec(memory_space=pl.ANY)
VMEM = pl.BlockSpec(memory_space=pltpu.VMEM)


def split16(count):
    first = -(-count // 32) * 16
    return first, count - first


def remote(src, dst, send_sem, recv_sem, target):
    return pltpu.make_async_remote_copy(
        src_ref=src, dst_ref=dst, send_sem=send_sem, recv_sem=recv_sem,
        device_id=target, device_id_type=MESH,
    )


def greet(targets):
    barrier = pltpu.get_barrier_semaphore()
    for target in targets:
        pl.semaphore_signal(barrier, inc=1, device_id=target, device_id_type=MESH)
    pl.semaphore_wait(barrier, len(targets))


def place():
    q, s = lax.axis_index("seq"), lax.axis_index("shard")
    return q, s


def xy_targets():
    q, s = place()
    x, y = q // NX, q % NX
    right_x, left_x = (x + 1) % NX, (x + NX - 1) % NX
    right_y, left_y = (y + 1) % NX, (y + NX - 1) % NX
    return (x, y), (
        ((right_x * NX + y, s), (left_x * NX + y, s)),
        ((x * NX + right_y, s), (x * NX + left_y, s)),
    )


class RingGather:
    def __init__(self, view, rows, me, targets, sems):
        self.view, self.me = view, me
        self.parts = split16(rows)
        self.right, self.left = targets
        self.sems = sems
        self.r, self.l, self.o = (me + 1) % NX, (me + NX - 1) % NX, (me + 2) % NX

    def copy(self, slot, part, index, target, src=None):
        view = self.view(slot, part)
        return remote(view if src is None else src, view, self.sems[0].at[index], self.sems[1].at[index], target)

    def start(self, src=None):
        self.copy(self.me, None, 0, self.right, src).start()
        self.copy(self.me, None, 1, self.left, src).start()

    def forward(self):
        self.copy(self.l, None, 0, self.right).wait_recv()
        if self.parts[0]:
            self.copy(self.l, 0, 2, self.right).start()
        self.copy(self.r, None, 1, self.left).wait_recv()
        if self.parts[1]:
            self.copy(self.r, 1, 3, self.left).start()

    def finish(self):
        if self.parts[0]:
            self.copy(self.o, 0, 2, self.right).wait_recv()
        if self.parts[1]:
            self.copy(self.o, 1, 3, self.left).wait_recv()

    def drain(self):
        self.copy(self.me, None, 0, self.right).wait_send()
        self.copy(self.me, None, 1, self.left).wait_send()
        if self.parts[0]:
            self.copy(self.l, 0, 2, self.right).wait_send()
        if self.parts[1]:
            self.copy(self.r, 1, 3, self.left).wait_send()


def plane_gather_body(shapes, refs):
    count = len(shapes)
    ins, outs = refs[:count], refs[count : 2 * count]
    local_sem, send_sem, recv_sem = refs[2 * count :]
    (x, y), targets = xy_targets()
    greet([t for pair in targets for t in pair])
    first, second, locals_ = [], [], []
    for i, (rows, _) in enumerate(shapes):
        cut = split16(rows)
        own = pltpu.make_async_copy(ins[i], outs[i].at[x, y], local_sem.at[i])
        own.start()
        locals_.append(own)
        for half in range(2):
            size, base = cut[half], 0 if half == 0 else cut[0]
            if not size:
                continue
            parts = split16(size)
            spans = {None: pl.ds(base, size), 0: pl.ds(base, parts[0]), 1: pl.ds(base + parts[0], parts[1])}
            out = outs[i]
            if half == 0:
                v1 = lambda k, part, out=out, spans=spans: out.at[k, y, spans[part]]
                v2 = lambda k, part, out=out, spans=spans: out.at[:, k, spans[part]]
                m1, m2, t1, t2 = x, y, targets[0], targets[1]
            else:
                v1 = lambda k, part, out=out, spans=spans: out.at[x, k, spans[part]]
                v2 = lambda k, part, out=out, spans=spans: out.at[k, :, spans[part]]
                m1, m2, t1, t2 = y, x, targets[1], targets[0]
            sems = [(send_sem.at[i, half, st], recv_sem.at[i, half, st]) for st in range(2)]
            first.append((RingGather(v1, size, m1, t1, sems[0]), ins[i].at[spans[None]]))
            second.append(RingGather(v2, size, m2, t2, sems[1]))
    for ring, src in first:
        ring.start(src)
    for ring, _ in first:
        ring.forward()
    for own in locals_:
        own.wait()
    for (ring, _), later in zip(first, second):
        ring.finish()
        later.start()
    for ring in second:
        ring.forward()
    for ring in second:
        ring.finish()
    for ring, _ in first:
        ring.drain()
    for ring in second:
        ring.drain()


def plane_gather(arrays, collective_id):
    shapes = [a.shape for a in arrays]

    def kernel(*refs):
        plane_gather_body(shapes, refs)

    count = len(arrays)
    return pl.pallas_call(
        kernel,
        out_shape=[jax.ShapeDtypeStruct((NX, NX) + a.shape, a.dtype) for a in arrays],
        in_specs=[ANY] * count,
        out_specs=[ANY] * count,
        scratch_shapes=[
            pltpu.SemaphoreType.DMA((count,)),
            pltpu.SemaphoreType.DMA((count, 2, 2, 4)),
            pltpu.SemaphoreType.DMA((count, 2, 2, 4)),
        ],
        compiler_params=pltpu.CompilerParams(collective_id=collective_id, has_side_effects=True),
    )(*arrays)


class RingSum:
    def __init__(self, view, lead, rows, me, targets, sems, bufs):
        self.view, self.lead, self.me = view, lead, me
        self.rows = rows
        self.parts = split16(rows)
        self.right, self.left = targets
        self.sems = sems
        self.acc, self.fin, self.plain = bufs
        self.r, self.l, self.o = (me + 1) % NX, (me + NX - 1) % NX, (me + 2) % NX

    def span(self, part):
        return pl.ds(0, self.parts[0]) if part == 0 else pl.ds(self.parts[0], self.parts[1])

    def buf(self, ref, part):
        return ref.at[:, self.span(part)]

    def copy(self, index):
        part = index % 2 if index < 2 or index >= 4 else 1 - index % 2
        target = self.right if index % 2 == 0 else self.left
        if index < 2:
            src, dst = self.view(self.o, part), self.buf(self.acc, part)
        elif index < 4:
            src, dst = self.view(self.r if index == 2 else self.l, part), self.buf(self.plain, part)
        else:
            src, dst = self.buf(self.acc, part), self.buf(self.fin, part)
        return remote(src, dst, self.sems[0].at[index], self.sems[1].at[index], target)

    def live(self, index):
        part = index % 2 if index < 2 or index >= 4 else 1 - index % 2
        return self.parts[part] > 0

    def start(self):
        for index in range(4):
            if self.live(index):
                self.copy(index).start()

    def middle(self):
        for index in range(2):
            if not self.live(index):
                continue
            self.copy(index).wait_recv()
            mine = self.view(self.r if index == 0 else self.l, index)
            buf = self.buf(self.acc, index)
            steps = self.parts[index] // 16

            def add(n, _, mine=mine, buf=buf, steps=steps):
                at = (n // steps, pl.ds(pl.multiple_of((n % steps) * 16, 16), 16))
                buf[at] = (buf[at].astype(F32) + mine[at].astype(F32)).astype(buf.dtype)
                return 0

            lax.fori_loop(0, self.lead * steps, add, 0)
            self.copy(4 + index).start()

    def finish(self, out):
        for index in range(2, 6):
            if self.live(index):
                self.copy(index).wait_recv()
        steps = self.rows // 16
        mine = self.view(self.me, None)

        def add(n, _):
            at = (n // steps, pl.ds(pl.multiple_of((n % steps) * 16, 16), 16))
            total = mine[at].astype(F32) + self.fin[at].astype(F32) + self.plain[at].astype(F32)
            out[at] = total.astype(out.dtype)
            return 0

        lax.fori_loop(0, self.lead * steps, add, 0)

    def drain(self):
        for index in range(6):
            if self.live(index):
                self.copy(index).wait_send()


def plane_sum_scratch(shapes):
    scratch = [
        pltpu.SemaphoreType.DMA((len(shapes), 2, 2, 6)),
        pltpu.SemaphoreType.DMA((len(shapes), 2, 2, 6)),
    ]
    for rows, width in shapes:
        for size in split16(rows):
            if size:
                scratch += [pltpu.VMEM((NX, size, width), BF)] * 4 + [pltpu.VMEM((1, size, width), BF)] * 3
    return scratch


def plane_sum_rings(shapes, ins, scratch):
    send_sem, recv_sem = scratch[:2]
    bufs = list(scratch[2:])
    (x, y), targets = xy_targets()
    rings = []
    for i, (rows, _) in enumerate(shapes):
        cut = split16(rows)
        for half in range(2):
            size, base = cut[half], 0 if half == 0 else cut[0]
            if not size:
                continue
            mine, bufs = bufs[:7], bufs[7:]
            parts = split16(size)
            spans = {None: pl.ds(base, size), 0: pl.ds(base, parts[0]), 1: pl.ds(base + parts[0], parts[1])}
            low = {None: pl.ds(0, size), 0: pl.ds(0, parts[0]), 1: pl.ds(parts[0], parts[1])}
            src, held = ins[i], mine[3]
            if half == 0:
                v1 = lambda k, part, src=src, spans=spans: src.at[k, :, spans[part]]
                m1, m2, t1, t2 = x, y, targets[0], targets[1]
            else:
                v1 = lambda k, part, src=src, spans=spans: src.at[:, k, spans[part]]
                m1, m2, t1, t2 = y, x, targets[1], targets[0]
            v2 = lambda k, part, held=held, low=low: held.at[pl.ds(k, 1), low[part]]
            sems = [(send_sem.at[i, half, st], recv_sem.at[i, half, st]) for st in range(2)]
            first = RingSum(v1, NX, size, m1, t1, sems[0], mine[:3])
            second = RingSum(v2, 1, size, m2, t2, sems[1], mine[4:7])
            rings.append((first, second, held, i, base, size))
    return rings


def plane_sum(arrays, collective_id):
    shapes = [a.shape[2:] for a in arrays]
    count = len(arrays)

    def kernel(*refs):
        ins, outs, scratch = refs[:count], refs[count : 2 * count], refs[2 * count :]
        _, targets = xy_targets()
        greet([t for pair in targets for t in pair])
        rings = plane_sum_rings(shapes, ins, scratch)
        for ring in rings:
            ring[0].start()
        for ring in rings:
            ring[0].middle()
        for first, second, held, *_ in rings:
            first.finish(held)
            second.start()
        for ring in rings:
            ring[1].middle()
        for _, second, _, i, base, size in rings:
            second.finish(outs[i].at[:, pl.ds(base, size)])
        for ring in rings:
            ring[0].drain()
            ring[1].drain()

    outs = pl.pallas_call(
        kernel,
        out_shape=[jax.ShapeDtypeStruct((1,) + s, F32) for s in shapes],
        in_specs=[VMEM] * count,
        out_specs=[VMEM] * count,
        scratch_shapes=plane_sum_scratch(shapes),
        compiler_params=pltpu.CompilerParams(
            collective_id=collective_id, has_side_effects=True, vmem_limit_bytes=60 << 20
        ),
    )(*arrays)
    return [o[0] for o in outs]


def z_targets():
    q, s = place()
    z, c = s // 2, s % 2
    up, down = (z + 1) % NZ, (z + NZ - 1) % NZ
    return z, c, (q, z * 2 + 1 - c), (q, up * 2 + c), (q, down * 2 + c)


def shard_gather(block, collective_id):
    rows, width = block.shape
    parts = split16(rows)

    def kernel(src, out, local_sem, send_sem, recv_sem):
        z, c, partner, up, down = z_targets()
        greet([partner, up, down])
        slot = lambda k, core: ((k + NZ) % NZ) * 2 + core
        span = (pl.ds(0, parts[0]), pl.ds(parts[0], parts[1]))
        mine = slot(z, c)

        def copy(index, view, target, source=None):
            return remote(view if source is None else source, view, send_sem.at[index], recv_sem.at[index], target)

        own = pltpu.make_async_copy(src, out.at[mine], local_sem)
        own.start()
        sends = [copy(0, out.at[mine], up, src), copy(1, out.at[mine], down, src), copy(2, out.at[mine], partner, src)]
        for send in sends:
            send.start()

        def go(*args):
            send = copy(*args)
            send.start()
            sends.append(send)

        from_down, from_up, far = slot(z - 1, c), slot(z + 1, c), slot(z + 2, c)
        copy(0, out.at[from_down], up).wait_recv()
        go(3, out.at[from_down, span[0]], up)
        go(5, out.at[from_down], partner)
        copy(1, out.at[from_up], down).wait_recv()
        go(4, out.at[from_up, span[1]], down)
        go(6, out.at[from_up], partner)
        copy(3, out.at[far, span[0]], up).wait_recv()
        go(7, out.at[far, span[0]], partner)
        copy(4, out.at[far, span[1]], down).wait_recv()
        go(8, out.at[far, span[1]], partner)
        copy(2, out.at[slot(z, 1 - c)], partner).wait_recv()
        copy(5, out.at[slot(z - 1, 1 - c)], partner).wait_recv()
        copy(6, out.at[slot(z + 1, 1 - c)], partner).wait_recv()
        copy(7, out.at[slot(z + 2, 1 - c), span[0]], partner).wait_recv()
        copy(8, out.at[slot(z + 2, 1 - c), span[1]], partner).wait_recv()
        own.wait()
        for send in sends:
            send.wait_send()

    return pl.pallas_call(
        kernel,
        out_shape=jax.ShapeDtypeStruct((NZ * 2, rows, width), block.dtype),
        in_specs=[ANY],
        out_specs=ANY,
        scratch_shapes=[
            pltpu.SemaphoreType.DMA,
            pltpu.SemaphoreType.DMA((9,)),
            pltpu.SemaphoreType.DMA((9,)),
        ],
        compiler_params=pltpu.CompilerParams(collective_id=collective_id, has_side_effects=True),
    )(block)


def shard_sum(terms, collective_id):
    _, rows, width = terms.shape
    parts = split16(rows)

    def kernel(src, out, met, acc, fin, plain, pair, send_sem, recv_sem):
        z, c, partner, up, down = z_targets()
        greet([partner, up, down])
        ring = lambda k: (k + NZ) % NZ
        span = (pl.ds(0, parts[0]), pl.ds(parts[0], parts[1]))
        sends = []

        def copy(index, source, target, dst):
            return remote(source, dst, send_sem.at[index], recv_sem.at[index], target)

        def go(*args):
            send = copy(*args)
            send.start()
            sends.append(send)

        order = (ring(z + 2), ring(z + 1), ring(z - 1), z)
        for i, k in enumerate(order):
            go(i, src.at[k * 2 + 1 - c], partner, met.at[k])

        def tiles(part, body):
            base = 0 if part == 0 else parts[0]

            def step(n, _):
                body(pl.ds(pl.multiple_of(base + n * 16, 16), 16))
                return 0

            lax.fori_loop(0, parts[part] // 16, step, 0)

        def both(k, at):
            return src[k * 2 + c, at] + met[k, at]

        def put(k, part, extra=None):
            def body(at):
                total = both(k, at)
                if extra is not None:
                    total = total + extra[at].astype(F32)
                pair[k, at] = total.astype(BF)

            tiles(part, body)

        def arrived(i):
            copy(i, src.at[0], partner, met.at[order[i]]).wait_recv()

        arrived(0)
        put(order[0], 0)
        go(4, pair.at[order[0], span[0]], up, acc.at[span[0]])
        put(order[0], 1)
        go(5, pair.at[order[0], span[1]], down, acc.at[span[1]])
        arrived(1)
        put(order[1], 1)
        go(6, pair.at[order[1], span[1]], up, plain.at[span[1]])
        arrived(2)
        put(order[2], 0)
        go(7, pair.at[order[2], span[0]], down, plain.at[span[0]])
        copy(4, acc.at[span[0]], up, acc.at[span[0]]).wait_recv()
        put(order[1], 0, acc)
        go(8, pair.at[order[1], span[0]], up, fin.at[span[0]])
        copy(5, acc.at[span[1]], down, acc.at[span[1]]).wait_recv()
        put(order[2], 1, acc)
        go(9, pair.at[order[2], span[1]], down, fin.at[span[1]])
        arrived(3)
        copy(6, plain.at[span[1]], up, plain.at[span[1]]).wait_recv()
        copy(7, plain.at[span[0]], down, plain.at[span[0]]).wait_recv()
        copy(8, fin.at[span[0]], up, fin.at[span[0]]).wait_recv()
        copy(9, fin.at[span[1]], down, fin.at[span[1]]).wait_recv()

        def last(at):
            out[at] = both(z, at) + fin[at].astype(F32) + plain[at].astype(F32)

        tiles(0, last)
        tiles(1, last)
        for send in sends:
            send.wait_send()

    return pl.pallas_call(
        kernel,
        out_shape=jax.ShapeDtypeStruct((rows, width), F32),
        in_specs=[VMEM],
        out_specs=VMEM,
        scratch_shapes=[
            pltpu.VMEM((NZ, rows, width), F32),
            pltpu.VMEM((rows, width), BF),
            pltpu.VMEM((rows, width), BF),
            pltpu.VMEM((rows, width), BF),
            pltpu.VMEM((NZ, rows, width), BF),
            pltpu.SemaphoreType.DMA((10,)),
            pltpu.SemaphoreType.DMA((10,)),
        ],
        compiler_params=pltpu.CompilerParams(
            collective_id=collective_id, has_side_effects=True, vmem_limit_bytes=40 << 20
        ),
    )(terms)


def seq_exchange(pair, collective_id, backward):
    count = NX * NX
    width = pair.shape[1]

    def kernel(src, out, slots, send_sem, recv_sem):
        q, s = place()
        peers = [((q + d) % count, s) for d in range(1, count)]
        greet(peers)
        sends = [remote(src, slots.at[d], send_sem.at[d], recv_sem.at[d], peers[d - 1]) for d in range(1, count)]
        for send in sends:
            send.start()
        for send in sends:
            send.wait_recv()
        state = jnp.zeros((1, width), F32)
        for step in range(1, count):
            d = step if backward else count - step
            seen = (q + count - d) % count
            use = seen > q if backward else seen < q
            value = slots[d, 1:2] + slots[d, 0:1] * state
            state = jnp.where(use, value, state)
        out[...] = jnp.broadcast_to(state, out.shape)
        for send in sends:
            send.wait_send()

    return pl.pallas_call(
        kernel,
        out_shape=jax.ShapeDtypeStruct((8, width), F32),
        in_specs=[VMEM],
        out_specs=VMEM,
        scratch_shapes=[
            pltpu.VMEM((count, 8, width), F32),
            pltpu.SemaphoreType.DMA((count,)),
            pltpu.SemaphoreType.DMA((count,)),
        ],
        compiler_params=pltpu.CompilerParams(collective_id=collective_id, has_side_effects=True),
    )(pair)


def small_sum(blocks, collective_id):
    count, _, width = blocks.shape

    def kernel(src, out, slots, total, others, send_sem, recv_sem):
        q, s = place()
        peers = [((q + d) % count, s) for d in range(1, count)]
        mates = [(q, (s + d) % 8) for d in range(1, 8)]
        greet(peers + mates)
        sends = [
            remote(src.at[(q + d) % count], slots.at[d], send_sem.at[d], recv_sem.at[d], peers[d - 1])
            for d in range(1, count)
        ]
        for send in sends:
            send.start()
        value = src[q]
        for d in range(1, count):
            sends[d - 1].wait_recv()
            value = value + slots[d]
        total[...] = value
        more = [
            remote(total, others.at[d], send_sem.at[count + d], recv_sem.at[count + d], mates[d - 1])
            for d in range(1, 8)
        ]
        for send in more:
            send.start()
        wide = value
        for d in range(1, 8):
            more[d - 1].wait_recv()
            wide = wide + others[d]
        out[...] = wide
        out[0:1] = value[0:1]
        for send in sends + more:
            send.wait_send()

    return pl.pallas_call(
        kernel,
        out_shape=jax.ShapeDtypeStruct((8, width), F32),
        in_specs=[VMEM],
        out_specs=VMEM,
        scratch_shapes=[
            pltpu.VMEM((count, 8, width), F32),
            pltpu.VMEM((8, width), F32),
            pltpu.VMEM((8, 8, width), F32),
            pltpu.SemaphoreType.DMA((count + 8,)),
            pltpu.SemaphoreType.DMA((count + 8,)),
        ],
        compiler_params=pltpu.CompilerParams(collective_id=collective_id, has_side_effects=True),
    )(blocks)


def local_scan(decay, inflow, backward=False):
    rows, width = decay.shape
    groups = rows // 8

    def kernel(a_ref, b_ref, prod_ref, state_ref):
        index = lax.broadcasted_iota(jnp.int32, (8, width), 0)

        def step(n, carry):
            prod, state = carry
            g = groups - 1 - n if backward else n
            at = pl.ds(pl.multiple_of(g * 8, 8), 8)
            a, b = a_ref[at], b_ref[at]
            for shift in (1, 2, 4):
                keep = index < 8 - shift if backward else index >= shift
                turn = 8 - shift if backward else shift
                a_far = jnp.where(keep, pltpu.roll(a, turn, 0), 1.0)
                b_far = jnp.where(keep, pltpu.roll(b, turn, 0), 0.0)
                a, b = a * a_far, a * b_far + b
            a, b = a * prod, a * state + b
            prod_ref[at] = a
            state_ref[at] = b
            end = slice(0, 1) if backward else slice(7, 8)
            return a[end], b[end]

        lax.fori_loop(0, groups, step, (jnp.ones((1, width), F32), jnp.zeros((1, width), F32)), unroll=4)

    return pl.pallas_call(
        kernel,
        out_shape=[jax.ShapeDtypeStruct((rows, width), F32)] * 2,
        in_specs=[VMEM] * 2,
        out_specs=[VMEM] * 2,
    )(decay, inflow)


def rms_scale(row_block, gain_row):
    return (
        row_block
        * lax.rsqrt(jnp.mean(row_block * row_block, axis=-1, keepdims=True) + norm_eps)
        * gain_row
    )


def gelu_fn(values):
    return jax.nn.gelu(values, approximate=True)


def gate_piece(conv_out, pre_decay, pre_input, lam_row, reset_mask):
    gate_decay = jax.nn.sigmoid(pre_decay)
    gate_input = jax.nn.sigmoid(pre_input)
    log_decay = -8.0 * gate_decay * jax.nn.softplus(lam_row)
    norm_scale = jnp.where(reset_mask > 0, 1.0, jnp.sqrt(-jnp.expm1(2.0 * log_decay)))
    return (jnp.exp(log_decay) * (1.0 - reset_mask), conv_out * gate_input * norm_scale)


def adam_step(weight, moment_one, moment_two, gradient, step_rate, weight_decay):
    first_new = beta_one * moment_one + (1.0 - beta_one) * gradient
    second_new = beta_two * moment_two + (1.0 - beta_two) * gradient * gradient
    bias_one = 1.0 - beta_one**STEP
    bias_two = 1.0 - beta_two**STEP
    update = (
        first_new / bias_one / (jnp.sqrt(second_new / bias_two) + adam_eps) + weight_decay * weight
    )
    return (first_new, second_new, weight - step_rate * update)


def contract(left_side, right_side, left_dim, right_dim):
    return lax.dot_general(
        left_side,
        right_side,
        (((left_dim,), (right_dim,)), ((), ())),
        preferred_element_type=F32,
    )


def tap_mask(positions, bounds):
    starts = jnp.max(jnp.where(bounds[None, :] <= positions[:, None], bounds[None, :], 0), axis=1)
    offsets = jnp.arange(CONV, dtype=jnp.int32)
    return (positions[:, None] - offsets[None, :] >= starts[:, None]).astype(F32)


def shards(
    tokens, cotangent, doc_bounds,
    branch_w, branch_m, branch_v, out_w, out_m, out_v, gate_w, gate_m, gate_v,
    mlp_w, mlp_m, mlp_v, down_w, down_m, down_v, chan_w, chan_m, chan_v, gains_w, gains_m, gains_v,
):
    T, D = tokens.shape
    NQ, NS = lax.axis_size("seq"), lax.axis_size("shard")
    q, s = lax.axis_index("seq"), lax.axis_index("shard")
    H, J = branch_w.shape[2:]
    C = H * J
    B = D // NQ
    F = mlp_w.shape[2]
    G16 = gate_w.shape[2]
    rows = T // NS

    wb = branch_w.astype(BF).reshape(2, B, C).transpose(1, 0, 2).reshape(B, 2 * C)
    wg = gate_w.astype(BF).transpose(2, 0, 1, 3).reshape(G16, 2 * C)
    wo = out_w.astype(BF).reshape(C, B).T
    wm0, wm1 = mlp_w[0].astype(BF), mlp_w[1].astype(BF)
    wd = down_w.astype(BF).T
    tiny = jnp.zeros((16, 256), BF)
    tiny = tiny.at[:8, : 2 * H].set(chan_w.astype(BF).reshape(8, 2 * H))
    tiny = tiny.at[8:10, :B].set(gains_w.astype(BF))
    last = tokens[T - 16 :]
    edge = lax.ppermute(last, "seq", [(i, i + 1) for i in range(NQ - 1)])
    wb, wg, wo, wm0, wm1, wd, tiny = plane_gather([wb, wg, wo, wm0, wm1, wd, tiny], 1)
    wb = wb.reshape(D, 2 * C)
    wo = wo.reshape(D, C)
    wm0, wm1 = wm0.reshape(D, F), wm1.reshape(D, F)
    wd = wd.reshape(D, F)
    tiny = tiny.reshape(NQ, 16, 256).astype(F32)
    chan = tiny[:, :8, : 2 * H].reshape(NQ, 8, H, 2).transpose(1, 2, 0, 3).reshape(8, C)
    gains = tiny[:, 8:10, :B].transpose(1, 0, 2).reshape(2, D)
    head_of = jnp.arange(2 * C, dtype=jnp.int32) // J % H
    same_head = (head_of[None, :] == jnp.arange(H, dtype=jnp.int32)[:, None]).astype(BF)
    wg = wg.reshape(NS, 1, J, 2 * C) * same_head[None, :, None, :]
    wg = wg.reshape(NS * C, 2 * C)

    positions = q * T + jnp.arange(T, dtype=jnp.int32)
    reset_mask = jnp.any(doc_bounds[None, :] == positions[:, None], axis=1).astype(F32)[:, None]
    taps = tap_mask(q * T + jnp.arange(T + CONV - 1, dtype=jnp.int32), doc_bounds)
    kernel = chan[0:CONV]

    ext = jnp.concatenate([edge, tokens], axis=0).astype(F32)
    normed_ext = rms_scale(ext, gains[0]).astype(BF)
    normed = normed_ext[16:]
    proj = jnp.dot(normed_ext, wb, preferred_element_type=F32)
    padded = proj[16 - CONV + 1 :, :C].astype(BF).astype(F32)
    branch_y = proj[16:, C:]
    conv_out = chan[CONV][None]
    for k in range(CONV):
        conv_out = conv_out + taps[:T, k, None] * kernel[k] * padded[CONV - 1 - k : CONV - 1 - k + T]
    gate_in = shard_gather(conv_out.astype(BF), 2)
    pre = jnp.zeros((T, 2 * C), F32)
    for k in range(NS):
        pre = pre + jnp.dot(gate_in[k], wg[k * C : (k + 1) * C], preferred_element_type=F32)
    (decay_rate, inflow), gate_back = jax.vjp(
        partial(gate_piece, reset_mask=reset_mask),
        conv_out,
        pre[:, :C] + chan[CONV + 1],
        pre[:, C:] + chan[CONV + 2],
        chan[CONV + 3],
    )
    cum_decay, local_state = local_scan(decay_rate, inflow)
    ends = jnp.concatenate([cum_decay[-1:], local_state[-1:], jnp.zeros((6, C), F32)], axis=0)
    carried = seq_exchange(ends, 3, False)[0:1]
    lru_state = local_state + cum_decay * carried
    gate_y, gate_y_back = jax.vjp(gelu_fn, branch_y)
    mixed_out = (lru_state * gate_y).astype(BF)
    part = contract(mixed_out, wo, 1, 1).reshape(NS, rows, D)
    my_tokens = lax.dynamic_slice_in_dim(tokens, s * rows, rows, 0).astype(F32)
    middle = my_tokens + shard_sum(part, 4)
    normed_two = shard_gather(rms_scale(middle, gains[1]).astype(BF), 5).reshape(T, D)

    gate_val = jnp.dot(normed_two, wm0, preferred_element_type=F32)
    up_val = jnp.dot(normed_two, wm1, preferred_element_type=F32)
    gate_act, gate_act_back = jax.vjp(gelu_fn, gate_val)
    hidden = (gate_act * up_val).astype(BF)
    d_hidden = jnp.dot(cotangent, wd, preferred_element_type=F32)
    d_gate = gate_act_back(d_hidden * up_val)[0].astype(BF)
    d_up = (d_hidden * gate_act).astype(BF)
    part = (contract(d_gate, wm0, 1, 1) + contract(d_up, wm1, 1, 1)).reshape(NS, rows, D)
    d_normed_two = shard_sum(part, 4)
    part = contract(hidden, wd, 1, 1).reshape(NS, rows, D)
    block_rows = (middle + shard_sum(part, 4)).astype(BF)
    block_out = shard_gather(block_rows, 5).reshape(T, D)
    d_down = contract(cotangent, hidden, 0, 0).astype(BF)
    d_mlp0 = contract(normed_two, d_gate, 0, 0).astype(BF)
    d_mlp1 = contract(normed_two, d_up, 0, 0).astype(BF)

    _, norm_two_back = jax.vjp(rms_scale, middle, gains[1])
    d_middle_norm, d_gain_two = norm_two_back(d_normed_two)
    my_cot = lax.dynamic_slice_in_dim(cotangent, s * rows, rows, 0).astype(F32)
    d_middle = my_cot + d_middle_norm
    d_middle_low = shard_gather(d_middle.astype(BF), 5).reshape(T, D)
    d_out = contract(d_middle_low, mixed_out, 0, 0).astype(BF)
    d_mixed = jnp.dot(d_middle_low, wo, preferred_element_type=F32)
    d_branch_y = gate_y_back(d_mixed * lru_state)[0].astype(BF)
    next_decay = jnp.concatenate([decay_rate[1:], jnp.ones_like(decay_rate[:1])], axis=0)
    reach, local_grad = local_scan(next_decay, d_mixed * gate_y, True)
    ends = jnp.concatenate(
        [decay_rate[0:1] * reach[0:1], decay_rate[0:1] * local_grad[0:1], jnp.zeros((6, C), F32)], axis=0
    )
    came_back = seq_exchange(ends, 6, True)[0:1]
    grad_state = local_grad + reach * came_back
    prev_state = jnp.concatenate([carried, lru_state[:-1]], axis=0)
    d_direct, d_pre_decay, d_pre_input, d_lam = gate_back((grad_state * prev_state, grad_state))
    d_pre_low = jnp.concatenate([d_pre_decay, d_pre_input], axis=1).astype(BF)
    d_gate_in = jnp.stack(
        [contract(d_pre_low, wg[k * C : (k + 1) * C], 1, 1) for k in range(NS)]
    )
    d_gate_in = shard_sum(d_gate_in, 7)
    d_gate_w = jnp.stack([contract(gate_in[k], d_pre_low, 0, 0) for k in range(NS)])
    d_gate_w = jnp.sum(d_gate_w.reshape(NS, H, J, 2 * C) * same_head[None, :, None, :].astype(F32), axis=1)
    d_gate_w = d_gate_w.astype(BF).reshape(NX, NX, G16, 2 * C)
    d_conv = (d_direct + d_gate_in).astype(BF)
    right_edge = lax.ppermute(d_conv[: CONV - 1], "seq", [(i + 1, i) for i in range(NQ - 1)])
    d_conv_ext = jnp.concatenate([d_conv, right_edge], axis=0).astype(F32)
    d_branch_x = jnp.zeros((T, C), F32)
    for k in range(CONV):
        d_branch_x = d_branch_x + kernel[k] * (taps[k : k + T, k, None] * d_conv_ext[k : k + T])
    d_branch_x = d_branch_x.astype(BF)
    d_conv_vals = d_conv_ext[:T]
    d_chan = jnp.stack(
        [
            jnp.sum(taps[:T, k, None] * d_conv_vals * padded[CONV - 1 - k : CONV - 1 - k + T], axis=0)
            for k in range(CONV)
        ]
        + [jnp.sum(d_conv_vals, axis=0), jnp.sum(d_pre_decay, axis=0), jnp.sum(d_pre_input, axis=0), d_lam]
    )
    d_proj = jnp.concatenate([d_branch_x, d_branch_y], axis=1)
    d_branch = contract(normed, d_proj, 0, 0).astype(BF)
    part = contract(d_proj, wb, 1, 1).reshape(NS, rows, D)
    d_normed = shard_sum(part, 4)
    _, norm_one_back = jax.vjp(rms_scale, my_tokens, gains[0])
    d_token_norm, d_gain_one = norm_one_back(d_normed)
    token_grad = shard_gather((d_middle + d_token_norm).astype(BF), 5).reshape(T, D).astype(F32)

    d_gains = jnp.stack([d_gain_one, d_gain_two])
    small = jnp.zeros((NQ, 8, 256), F32)
    small = small.at[:, 0, : 16 * H].set(
        d_chan.reshape(8, H, NQ, 2).transpose(2, 0, 1, 3).reshape(NQ, 16 * H)
    )
    small = small.at[:, 1:3, :B].set(d_gains.reshape(2, NQ, B).transpose(1, 0, 2))
    small = small_sum(small, 8)
    red_chan = small[0, : 16 * H].reshape(8, H, 2)
    red_gains = small[1:3, :B]
    grid = lambda g: g.reshape(NX, NX, B, g.shape[1])
    red_mlp0, red_mlp1, red_down = plane_sum([grid(d_mlp0), grid(d_mlp1), grid(d_down)], 9)
    red_branch, red_out, red_gate = plane_sum([grid(d_branch), grid(d_out), d_gate_w], 10)
    red_branch = red_branch.reshape(B, 2, C).transpose(1, 0, 2).reshape(2, B, H, J)
    red_out = red_out.T.reshape(H, J, B)
    red_gate = red_gate.reshape(G16, 2, H, J).transpose(1, 2, 0, 3)
    red_mlp = jnp.stack([red_mlp0, red_mlp1])
    red_down = red_down.T
    branch_res = adam_step(branch_w, branch_m, branch_v, red_branch, matrix_rate, matrix_decay)
    out_res = adam_step(out_w, out_m, out_v, red_out, matrix_rate, matrix_decay)
    gate_res = adam_step(gate_w, gate_m, gate_v, red_gate, matrix_rate, matrix_decay)
    mlp_res = adam_step(mlp_w, mlp_m, mlp_v, red_mlp, matrix_rate, matrix_decay)
    down_res = adam_step(down_w, down_m, down_v, red_down, matrix_rate, matrix_decay)
    chan_res = adam_step(chan_w, chan_m, chan_v, red_chan, vector_rate, 0.0)
    gains_res = adam_step(gains_w, gains_m, gains_v, red_gains, gain_rate, 0.0)
    return (
        (block_out, token_grad)
        + branch_res + out_res + gate_res + mlp_res + down_res + chan_res + gains_res
    )


def solution(mesh):
    branch, out, gate = P(None, "seq", None, "shard"), P(None, "shard", "seq"), P(None, None, "seq", "shard")
    mlp, down = P(None, "seq", "shard"), P("shard", "seq")
    chan, gains = P(None, None, ("shard", "seq")), P(None, "seq")
    params = [spec for one in (branch, out, gate, mlp, down, chan, gains) for spec in (one,) * 3]
    return jax.shard_map(
        shards,
        mesh=mesh,
        in_specs=(P("seq", None), P("seq", None), P(), *params),
        out_specs=(P("seq", None), P("seq", None), *params),
        check_vma=False,
    )
```
